512 devices in a mesh: row: 32 (over y, x), col: 16 (over z, core).
Axes of the slice: x: 4, y: 8, z: 8, core: 2. Of those that a mesh axis runs over, the one named last changes fastest.
Arguments:
- front: float32 [2, 8192, 8192], P(None, 'row', 'col'), may hold values from -6 to 6
- panel: float32 [2, 8192, 256], P(None, ('row', 'col')), may hold values from -1.5 to 1.5
- inverses: float32 [2, 2, 128, 128], replicated, may hold values from -2 to 2
- coupling: float32 [2, 128, 128], replicated, may hold values from -0.5 to 0.5
- channels: float32 [2, 8192, 512], P(None, ('row', 'col')), may hold values from -0.0625 to 0.0625
Outputs:
- schur: float32 [2, 8192, 8192], P(None, 'row', 'col')
- projected: float32 [2, 512, 512], replicated
The draws below stay inside these ranges and needn't reach their ends.
All inputs are finite; a program needn't handle non-finite values.
Results may differ from the reference program's by a relative error of at most 0.00016.
Values sent between devices are 32-bit elements; how exact they have to be, the bound alone decides.
A program may use at most 64 MiB of HBM per device.

```python
import jax
import jax.numpy as jnp
from jax import lax

M = 8192
K = 128
CH = 512


def draw_inverses(key, part):
    first_key, second_key = jax.random.split(jax.random.fold_in(key, 17))
    spread = jax.random.normal(first_key, (2, 2, K, K), jnp.float32) * (0.5 / jnp.sqrt(K * 1.0))
    spread = jnp.clip(spread, -0.9, 0.9)
    scales = jax.random.uniform(second_key, (2, 1, 1, 1), jnp.float32, 0.6, 1.4)
    identity = jnp.eye(K, dtype=jnp.float32)
    realpart = jnp.stack([identity, jnp.zeros_like(identity)])[None]
    return realpart * scales + spread


def block_scale(rng, extent, shards, smallest, largest):
    def one(axis_at, shards_of):
        steps = jax.random.uniform(jax.random.fold_in(jax.random.fold_in(rng, 6), axis_at), (shards_of,), jnp.float32, smallest / len(shards), largest / len(shards))
        return jnp.repeat(jnp.exp(steps), extent[axis_at] // shards_of).reshape((-1,) + (1,) * (len(extent) - axis_at - 1))

    loudness = one(*shards[0])
    for cut in shards[1:]:
        loudness = loudness * one(*cut)
    return loudness


def scatter_about(stream_key, extent, deviation, reach, pieces=(), kind=jnp.bfloat16):
    drawn = deviation * jax.random.normal(stream_key, extent, jnp.float32)
    if pieces:
        drawn = drawn * block_scale(stream_key, extent, pieces, -0.22, 0.18)
    return jnp.clip(drawn, -reach, reach).astype(kind)


def setup_inputs(seed: int = 0) -> dict:
    seeds = jax.random.split(jax.random.key(seed), 6)
    return {
        "front": scatter_about(seeds[0], (2, M, M), 1.0, 6.0, ((1, 32), (2, 16)), jnp.float32),
        "panel": scatter_about(seeds[1], (2, M, 2 * K), 0.25, 1.5, ((1, 512),), jnp.float32),
        "inverses": draw_inverses(jax.random.fold_in(seeds[5], 71), 0),
        "coupling": scatter_about(seeds[3], (2, K, K), K ** -0.5, 0.5, (), jnp.float32),
        "channels": scatter_about(seeds[4], (2, M, CH), M ** -0.5, 0.0625, ((1, 512),), jnp.float32),
    }


HIGH = lax.Precision.HIGHEST


def real_dot(left, right):
    return jnp.dot(left, right, precision=HIGH, preferred_element_type=jnp.float32)


def complex_dot(left, right):
    return jnp.stack([real_dot(left[0], right[0]) - real_dot(left[1], right[1]), real_dot(left[0], right[1]) + real_dot(left[1], right[0])])


def complex_dot_nt(left, right):
    return complex_dot(left, jnp.swapaxes(right, 1, 2))


def complex_dot_tn(left, right):
    return complex_dot(jnp.swapaxes(left, 1, 2), right)


def reference(front, panel, inverses, coupling, channels):
    first = panel[:, :, :K]
    second = panel[:, :, K:] - complex_dot(first, complex_dot_nt(inverses[0], coupling))
    columns = jnp.concatenate([first, second], axis=2)
    scaled = jnp.concatenate([complex_dot(first, inverses[0]), complex_dot(second, inverses[1])], axis=2)
    schur = front - complex_dot_nt(scaled, columns)
    projected = complex_dot_tn(channels, complex_dot(schur, channels))
    return schur, projected
```

```python
import functools

import jax
import jax.numpy as jnp
from jax import lax
from jax.experimental import pallas as pl
from jax.experimental.pallas import tpu as pltpu
from jax.sharding import PartitionSpec as P

MESH = pl.DeviceIdType.MESH
HIGH = lax.Precision.HIGHEST
F32 = jnp.float32
BF16 = jnp.bfloat16
NY, NX, NZ = 8, 4, 8
PA, PC = 2, 4
NP = PA + PC
L = 128
ORDERS = ("yxz", "xyz", "xyz", "xyz")


def split(v):
    hi = v.astype(BF16)
    return hi, (v - hi.astype(F32)).astype(BF16)


def bdot(a, b, nt=False):
    dims = (((1,), (1 if nt else 0,)), ((), ()))
    return lax.dot_general(a, b, dims, preferred_element_type=F32)


def dot3(a, b, nt=False):
    (ah, al), (bh, bl) = a, b
    return bdot(ah, bh, nt) + (bdot(ah, bl, nt) + bdot(al, bh, nt))


def hdot(a, b, nt=False):
    dims = (((1,), (1 if nt else 0,)), ((), ()))
    return lax.dot_general(a, b, dims, precision=HIGH, preferred_element_type=F32)


def chdot(a, b, nt=False):
    (ar, ai), (br, bi) = a, b
    return (
        hdot(ar, br, nt) - hdot(ai, bi, nt),
        hdot(ar, bi, nt) + hdot(ai, br, nt),
    )


def kernel(
    front_hbm, panel, inverses, coupling, channels, schur_hbm, proj_hbm,
    front, schur, own, ybuf, col, row, s_hi, s_lo, ct_hi, ct_lo, x_hi, x_lo,
    part, sib_in, acc1, in1, acc2, in2, acc3, in3, whole,
    y_s, y_r, z_s, z_r, x_s, x_r, c_s, c_r, w_s, w_r, wc_s, wc_r,
    ps_s, ps_r, r1_s, r1_r, r2_s, r2_r, e_s, e_r, g2_s, g2_r, g1_s, g1_r, f_s, f_r, local_sem,
):
    r = lax.axis_index("row")
    c = lax.axis_index("col")
    y, x, z, k = r // NX, lax.rem(r, NX), c // 2, lax.rem(c, 2)
    other = 1 - k

    def at(yy, xx, zz, kk):
        return (yy * NX + xx, zz * 2 + kk)

    def up(v, d, n):
        return lax.rem(v + (d + n), n)

    def peer(axis, d):
        if axis == "y":
            return at(up(y, d, NY), x, z, k)
        if axis == "x":
            return at(y, up(x, d, NX), z, k)
        return at(y, x, up(z, d, NZ), k)

    sibling = at(y, x, z, other)
    index = {"y": y, "x": x, "z": z}
    size = {"y": NY, "x": NX, "z": NZ}
    sent = []

    def send(src, dst, s, r_, dev):
        copy = pltpu.make_async_remote_copy(
            src_ref=src, dst_ref=dst, send_sem=s, recv_sem=r_, device_id=dev, device_id_type=MESH
        )
        copy.start()
        return copy

    def arrived(ref, sem):
        pltpu.make_async_copy(ref, ref, sem).wait()

    barrier = pltpu.get_barrier_semaphore()
    greeted = [sibling]
    greeted += [peer("y", d) for d in range(1, NY)]
    greeted += [peer("z", d) for d in range(1, NZ)]
    greeted += [peer("x", d) for d in range(1, NX)]
    for dev in greeted:
        pl.semaphore_signal(barrier, inc=1, device_id=dev, device_id_type=MESH)

    load_front = pltpu.make_async_copy(front_hbm, front, local_sem.at[0])
    load_front.start()
    for p in range(NP):
        if p < PA:
            own[p] = panel[:, :, p * L : (p + 1) * L]
        else:
            own[p] = channels[:, :, (p - PA) * L : (p - PA + 1) * L]
    pl.semaphore_wait(barrier, len(greeted))

    near_first = (1, 7, 2, 6, 3, 5, 4)
    on_diagonal = y == z

    def y_send(p):
        @pl.when(on_diagonal)
        def _():
            for d in near_first:
                send(own.at[p], col.at[p, x, :, z, k], y_s.at[p, d], y_r.at[p, d], peer("y", d))
            pltpu.make_async_copy(own.at[p], col.at[p, x, :, z, k], local_sem.at[1 + p]).start()

        @pl.when(jnp.logical_not(on_diagonal))
        def _():
            for d in near_first:
                send(own.at[p], ybuf.at[p, y], y_s.at[p, d], y_r.at[p, d], peer("y", d))
            send(own.at[p], col.at[p, x, :, z, k], z_s.at[p, y], z_r.at[p, z], at(y, x, y, k))

    def y_drain(p):
        for d in near_first:
            arrived(own.at[p], y_s.at[p, d])

    def z_step(p):
        for d in near_first:
            yy = up(y, -d, NY)
            arrived(own.at[p], y_r.at[p, d])

            @pl.when(yy != z)
            def _():
                send(ybuf.at[p, yy], col.at[p, x, :, z, k], z_s.at[p, yy], z_r.at[p, z], at(y, x, yy, k))

    def z_drain(p):
        for yy in range(NY):
            @pl.when(yy != z)
            def _():
                arrived(own.at[p], z_s.at[p, yy])

    right, left = up(x, 1, NX), up(x, -1, NX)

    def x_step(p):
        for d in (1, 7, 2, 6, 3, 5, 4):
            arrived(own.at[p], z_r.at[p, up(z, -d, NZ)])

        @pl.when(on_diagonal)
        def _():
            pltpu.make_async_copy(own.at[p], own.at[p], local_sem.at[1 + p]).wait()

        line = col.at[p, x, :, :, k]
        send(line, line, x_s.at[p, 0], x_r.at[p, 0], peer("x", 1))
        send(line, line, x_s.at[p, 1], x_r.at[p, 1], peer("x", -1))

    def half(p, xx, h):
        return col.at[p, xx, :, pl.ds(h * (NZ // 2), NZ // 2), k]

    def x_forward(p):
        arrived(col.at[p, left, :, :, k], x_r.at[p, 0])
        send(half(p, left, 0), half(p, left, 0), x_s.at[p, 2], x_r.at[p, 2], peer("x", 1))
        arrived(col.at[p, right, :, :, k], x_r.at[p, 1])
        send(half(p, right, 1), half(p, right, 1), x_s.at[p, 3], x_r.at[p, 3], peer("x", -1))

    def x_drain(p):
        for n in range(2):
            arrived(col.at[p, x, :, :, k], x_s.at[p, n])
            arrived(half(p, x, 0), x_s.at[p, 2 + n])

    def pair(p, kk):
        return col.at[p, pl.ds(2 * (1 - kk), 2), :, :, kk]

    def sib_step(p):
        arrived(half(p, x, 0), x_r.at[p, 2])
        arrived(half(p, x, 1), x_r.at[p, 3])
        send(pair(p, k), pair(p, k), c_s.at[p], c_r.at[p], sibling)

    def sib_wait(p):
        arrived(pair(p, other), c_r.at[p])

    def sib_drain(p):
        arrived(pair(p, k), c_s.at[p])

    spans = (pl.ds(0, PA), pl.ds(PA, PC))

    def row_part(g, zz, comp=None):
        if comp is None:
            return row.at[spans[g], :, zz, k]
        return row.at[spans[g], comp, zz, k]

    def row_own(g):
        pltpu.make_async_copy(own.at[spans[g]], row_part(g, z), local_sem.at[8 + g]).start()
        send(own.at[spans[g]], row_part(g, z), w_s.at[g, 0, 0], w_r.at[g, 0, 0], peer("z", 1))
        send(own.at[spans[g]], row_part(g, z), w_s.at[g, 0, 1], w_r.at[g, 0, 1], peer("z", -1))

    def row_ring(g, step):
        for way, sign in ((0, 1), (1, -1)):
            zz = up(z, -sign * step, NZ)
            arrived(row_part(g, zz), w_r.at[g, step - 1, way])
            comp = way if step == 3 else None
            part_ = row_part(g, zz, comp)
            send(part_, part_, w_s.at[g, step, way], w_r.at[g, step, way], peer("z", sign))

    def row_sib(g):
        for way in (0, 1):
            arrived(row_part(g, up(z, 4, NZ), way), w_r.at[g, 3, way])
        pltpu.make_async_copy(own.at[spans[g]], row_part(g, z), local_sem.at[8 + g]).wait()
        both = row.at[spans[g], :, :, k]
        send(both, both, wc_s.at[g], wc_r.at[g], sibling)

    def row_wait(g):
        arrived(row.at[spans[g], :, :, other], wc_r.at[g])

    def row_drain(g):
        for step in range(4):
            for way in (0, 1):
                comp = way if step == 3 else None
                arrived(row_part(g, z, comp), w_s.at[g, step, way])
        arrived(row.at[spans[g], :, :, k], wc_s.at[g])

    def make_g():
        inv0 = (inverses[0, 0], inverses[0, 1])
        inv1 = (inverses[1, 0], inverses[1, 1])
        m = chdot(inv0, (coupling[0], coupling[1]), nt=True)
        n = chdot(m, inv1)
        nm = chdot(n, m, nt=True)
        im = chdot(inv1, m, nt=True)

        def block(i):
            top = jnp.concatenate([inv0[i] + nm[i], -n[i]], axis=1)
            return jnp.concatenate([top, jnp.concatenate([-im[i], inv1[i]], axis=1)], axis=0)

        gr, gi = block(0), block(1)
        return jnp.concatenate(
            [jnp.concatenate([gr, gi], axis=1), jnp.concatenate([-gi, gr], axis=1)], axis=0
        )

    def row_cat():
        parts = [row[p, i].reshape(NZ * 2 * 16, L) for i in range(2) for p in range(PA)]
        return jnp.concatenate(parts, axis=1)

    def make_scaled(g):
        scaled = hdot(row_cat(), g)
        xr, xi = scaled[:, : PA * L], scaled[:, PA * L :]
        both = jnp.concatenate(
            [jnp.concatenate([xr, -xi], axis=1), jnp.concatenate([xi, xr], axis=1)], axis=0
        )
        x_hi[...], x_lo[...] = split(both)

    def make_schur():
        for l in range(2):
            xx = 2 * k + l
            parts = [col[p, xx, i].reshape(256, L) for i in range(2) for p in range(PA)]
            a = split(jnp.concatenate(parts, axis=1))
            update = dot3((x_hi[...], x_lo[...]), a, nt=True)
            for i in range(2):
                s = front[i, :, l * 256 : (l + 1) * 256] - update[i * 256 : (i + 1) * 256]
                schur[i, :, l * 256 : (l + 1) * 256] = s
                hi, lo = split(s)
                s_hi[i * 256 : (i + 1) * 256, l * 256 : (l + 1) * 256] = hi
                s_lo[i * 256 : (i + 1) * 256, l * 256 : (l + 1) * 256] = lo

    def make_ct():
        for i in range(2):
            for j in range(PC):
                t = row[PA + j, i].reshape(256, L).T
                hi, lo = split(t)
                ct_hi[i * 512 + j * L : i * 512 + (j + 1) * L] = hi
                ct_lo[i * 512 + j * L : i * 512 + (j + 1) * L] = lo

    def make_part(j):
        p = PA + j
        lines = []
        for l in range(2):
            xx = 2 * k + l
            lines.append(jnp.concatenate([col[p, xx, i].reshape(256, L) for i in range(2)], axis=1))
        b = split(jnp.concatenate(lines, axis=0))
        t = dot3((s_hi[...], s_lo[...]), b)
        ar = t[:256, :L] - t[256:, L:]
        ai = t[:256, L:] + t[256:, :L]
        q = dot3((ct_hi[...], ct_lo[...]), split(jnp.concatenate([ar, ai], axis=1)))
        part[j, 0] = q[:512, :L] - q[512:, L:]
        part[j, 1] = q[:512, L:] + q[512:, :L]

    def p_sib(j):
        send(part.at[j, other], sib_in.at[j], ps_s.at[j], ps_r.at[j], sibling)

    def dims(j):
        a, b, e = ORDERS[j]
        return a, b, e, 512 // size[a], 512 // size[a] // size[b]

    def rs1(j):
        a, b, e, h1, h2 = dims(j)
        arrived(sib_in.at[j], ps_r.at[j])
        acc1[j] = part[j, k] + sib_in[j]
        for d in range(1, size[a]):
            to = up(index[a], d, size[a])
            send(
                acc1.at[j, pl.ds(to * h1, h1)], in1.at[j, pl.ds(d * h1, h1)],
                r1_s.at[j, d], r1_r.at[j, d], peer(a, d),
            )

    def rs2(j):
        a, b, e, h1, h2 = dims(j)
        total = acc1[j, pl.ds(index[a] * h1, h1)]
        for d in range(1, size[a]):
            arrived(in1.at[j, pl.ds(d * h1, h1)], r1_r.at[j, d])
            total = total + in1[j, d * h1 : (d + 1) * h1]
        acc2[j, :h1] = total
        for d in range(1, size[b]):
            to = up(index[b], d, size[b])
            send(
                acc2.at[j, pl.ds(to * h2, h2)], in2.at[j, pl.ds(d * h2, h2)],
                r2_s.at[j, d], r2_r.at[j, d], peer(b, d),
            )

    def exchange(j):
        a, b, e, h1, h2 = dims(j)
        total = acc2[j, pl.ds(index[b] * h2, h2)]
        for d in range(1, size[b]):
            arrived(in2.at[j, pl.ds(d * h2, h2)], r2_r.at[j, d])
            total = total + in2[j, d * h2 : (d + 1) * h2]
        in3[j, index[e], :h2] = total
        mine = in3.at[j, index[e], pl.ds(0, h2)]
        for d in range(1, size[e]):
            send(mine, mine, e_s.at[j, d], e_r.at[j, d], peer(e, d))

    def ag2(j):
        a, b, e, h1, h2 = dims(j)
        for d in range(1, size[e]):
            arrived(in3.at[j, up(index[e], -d, size[e]), pl.ds(0, h2)], e_r.at[j, d])
        total = in3[j, 0, :h2]
        for i in range(1, size[e]):
            total = total + in3[j, i, :h2]
        start = index[a] * h1 + index[b] * h2
        whole[j, k, pl.ds(start, h2)] = total
        mine = whole.at[j, k, pl.ds(start, h2)]
        for d in range(1, size[b]):
            send(mine, mine, g2_s.at[j, d], g2_r.at[j, d], peer(b, d))

    def ag1(j):
        a, b, e, h1, h2 = dims(j)
        for d in range(1, size[b]):
            frm = up(index[b], -d, size[b])
            arrived(whole.at[j, k, pl.ds(index[a] * h1 + frm * h2, h2)], g2_r.at[j, d])
        mine = whole.at[j, k, pl.ds(index[a] * h1, h1)]
        for d in range(1, size[a]):
            send(mine, mine, g1_s.at[j, d], g1_r.at[j, d], peer(a, d))

    def out(j, kk):
        return pltpu.make_async_copy(
            whole.at[j, kk], proj_hbm.at[kk, :, pl.ds(j * L, L)], local_sem.at[11 + 2 * j + kk]
        )

    def fin(j):
        a, b, e, h1, h2 = dims(j)
        for d in range(1, size[a]):
            frm = up(index[a], -d, size[a])
            arrived(whole.at[j, k, pl.ds(frm * h1, h1)], g1_r.at[j, d])
        send(whole.at[j, k], whole.at[j, k], f_s.at[j], f_r.at[j], sibling)

    def fin_wait(j):
        arrived(whole.at[j, other], f_r.at[j])
        for kk in range(2):
            out(j, kk).start()

    def sum_drain(j):
        a, b, e, h1, h2 = dims(j)
        arrived(sib_in.at[j], ps_s.at[j])
        arrived(sib_in.at[j], f_s.at[j])
        for d in range(1, size[a]):
            arrived(in1.at[j, pl.ds(0, h1)], r1_s.at[j, d])
            arrived(in1.at[j, pl.ds(0, h1)], g1_s.at[j, d])
        for d in range(1, size[b]):
            arrived(in1.at[j, pl.ds(0, h2)], r2_s.at[j, d])
            arrived(in1.at[j, pl.ds(0, h2)], g2_s.at[j, d])
        for d in range(1, size[e]):
            arrived(in1.at[j, pl.ds(0, h2)], e_s.at[j, d])

    y_send(0)
    row_own(0)
    y_send(1)
    row_own(1)
    for p in range(2, NP):
        y_send(p)
    g = make_g()
    z_step(0)
    row_ring(0, 1)
    z_step(1)
    row_ring(0, 2)
    x_step(0)
    row_ring(0, 3)
    row_ring(1, 1)
    z_step(2)
    x_step(1)
    x_forward(0)
    row_sib(0)
    z_step(3)
    row_ring(1, 2)
    x_step(2)
    x_forward(1)
    sib_step(0)
    row_wait(0)
    make_scaled(g)
    z_step(4)
    row_ring(1, 3)
    x_step(3)
    x_forward(2)
    sib_step(1)
    z_step(5)
    x_step(4)
    row_sib(1)
    load_front.wait()
    sib_wait(0)
    sib_wait(1)
    make_schur()
    store_schur = pltpu.make_async_copy(schur, schur_hbm, local_sem.at[10])
    store_schur.start()
    row_wait(1)
    make_ct()
    x_forward(3)
    sib_step(2)
    x_step(5)
    x_forward(4)
    sib_step(3)
    sib_wait(2)
    make_part(0)
    p_sib(0)
    x_forward(5)
    sib_step(4)
    sib_wait(3)
    make_part(1)
    p_sib(1)
    rs1(0)
    sib_step(5)
    sib_wait(4)
    make_part(2)
    p_sib(2)
    rs2(0)
    rs1(1)
    sib_wait(5)
    make_part(3)
    p_sib(3)
    exchange(0)
    rs2(1)
    rs1(2)

    ag2(0)
    exchange(1)
    rs2(2)
    rs1(3)

    ag1(0)
    ag2(1)
    exchange(2)
    rs2(3)

    fin(0)
    ag1(1)
    ag2(2)
    exchange(3)

    fin_wait(0)
    fin(1)
    ag1(2)
    ag2(3)

    fin_wait(1)
    fin(2)
    ag1(3)

    fin_wait(2)
    fin(3)
    fin_wait(3)

    for p in range(NP):
        y_drain(p)
        z_drain(p)
        x_drain(p)
        sib_drain(p)
    for q in range(2):
        row_drain(q)
    for j in range(PC):
        sum_drain(j)
    store_schur.wait()
    for j in range(PC):
        for kk in range(2):
            out(j, kk).wait()


def local(front, panel, inverses, coupling, channels):
    any_, vmem = pl.BlockSpec(memory_space=pl.ANY), pl.BlockSpec(memory_space=pltpu.VMEM)
    dma = pltpu.SemaphoreType.DMA
    v = pltpu.VMEM
    scratch = [
        v((2, 256, 512), F32),
        v((2, 256, 512), F32),
        v((NP, 2, 16, L), F32),
        v((NP, NY, 2, 16, L), F32),
        v((NP, NX, 2, NZ, 2, 16, L), F32),
        v((NP, 2, NZ, 2, 16, L), F32),
        v((512, 512), BF16), v((512, 512), BF16),
        v((1024, 256), BF16), v((1024, 256), BF16),
        v((512, 512), BF16), v((512, 512), BF16),
        v((PC, 2, 512, L), F32),
        v((PC, 512, L), F32),
        v((PC, 512, L), F32), v((PC, 512, L), F32),
        v((PC, 128, L), F32), v((PC, 128, L), F32),
        v((PC, 8, L), F32), v((PC, 8, 16, L), F32),
        v((PC, 2, 512, L), F32),
        dma((NP, 8)), dma((NP, 8)), dma((NP, 8)), dma((NP, 8)),
        dma((NP, 4)), dma((NP, 4)), dma((NP,)), dma((NP,)),
        dma((2, 4, 2)), dma((2, 4, 2)), dma((2,)), dma((2,)),
        dma((PC,)), dma((PC,)),
        dma((PC, 8)), dma((PC, 8)), dma((PC, 8)), dma((PC, 8)),
        dma((PC, 8)), dma((PC, 8)), dma((PC, 8)), dma((PC, 8)),
        dma((PC, 8)), dma((PC, 8)), dma((PC,)), dma((PC,)),
        dma((20,)),
    ]
    return pl.pallas_call(
        kernel,
        out_shape=(
            jax.ShapeDtypeStruct((2, 256, 512), F32),
            jax.ShapeDtypeStruct((2, 512, 512), F32),
        ),
        in_specs=[any_, vmem, vmem, vmem, vmem],
        out_specs=(any_, any_),
        scratch_shapes=scratch,
        compiler_params=pltpu.CompilerParams(
            collective_id=0, has_side_effects=True, vmem_limit_bytes=48 * 2**20
        ),
        cost_estimate=pl.CostEstimate(flops=4 * 10**9, bytes_accessed=8 * 2**20, transcendentals=0),
    )(front, panel, inverses, coupling, channels)


def solution(mesh):
    in_specs = (P(None, "row", "col"), P(None, ("row", "col"), None), P(), P(), P(None, ("row", "col"), None))
    out_specs = (P(None, "row", "col"), P())
    return jax.shard_map(local, mesh=mesh, in_specs=in_specs, out_specs=out_specs, check_vma=False)
```

```python
import functools

import jax
import jax.numpy as jnp
from jax import lax
from jax.experimental import pallas as pl
from jax.experimental.pallas import tpu as pltpu
from jax.sharding import PartitionSpec as P

MESH = pl.DeviceIdType.MESH
HIGH = lax.Precision.HIGHEST
F32 = jnp.float32
BF16 = jnp.bfloat16
NY, NX, NZ = 8, 4, 8
PA, PC = 2, 4
NP = PA + PC
L = 128
PLANES = ("y", "z")
MEMBERS = 32
SLICE = 256 // MEMBERS


def split(v):
    hi = v.astype(BF16)
    return hi, (v - hi.astype(F32)).astype(BF16)


def bdot(a, b, nt=False):
    dims = (((1,), (1 if nt else 0,)), ((), ()))
    return lax.dot_general(a, b, dims, preferred_element_type=F32)


def dot3(a, b, nt=False):
    (ah, al), (bh, bl) = a, b
    return bdot(ah, bh, nt) + (bdot(ah, bl, nt) + bdot(al, bh, nt))


def hdot(a, b, nt=False):
    dims = (((1,), (1 if nt else 0,)), ((), ()))
    return lax.dot_general(a, b, dims, precision=HIGH, preferred_element_type=F32)


def chdot(a, b, nt=False):
    (ar, ai), (br, bi) = a, b
    return (
        hdot(ar, br, nt) - hdot(ai, bi, nt),
        hdot(ar, bi, nt) + hdot(ai, br, nt),
    )


def kernel(
    front_hbm, panel_hbm, inverses_hbm, coupling_hbm, channels_hbm, schur_hbm, proj_hbm,
    front, schur, inverses, coupling, own, mine, col, row, s_hi, s_lo, ct_hi, ct_lo, x_hi, x_lo,
    part, sib_in, acc, scat, exch, whole,
    g_s, g_r, x_s, x_r, f_s, w_s, w_r, wc_s, wc_r,
    ps_s, ps_r, rs_s, rs_r, e_s, e_r, ag_s, ag_r, fin_s, fin_r, local_sem, out_sem,
):
    r = lax.axis_index("row")
    c = lax.axis_index("col")
    y, x, z, k = r // NX, lax.rem(r, NX), c // 2, lax.rem(c, 2)
    other = 1 - k

    def at(yy, xx, zz, kk):
        return (yy * NX + xx, zz * 2 + kk)

    def up(v, d, n):
        return lax.rem(v + (d + n), n)

    sibling = at(y, x, z, other)
    user = x // 2
    odd = lax.rem(x, 2)
    on_diagonal = y == z

    def send(src, dst, s, r_, dev):
        copy = pltpu.make_async_remote_copy(
            src_ref=src, dst_ref=dst, send_sem=s, recv_sem=r_, device_id=dev, device_id_type=MESH
        )
        copy.start()

    def bring(src, dst, sem):
        pltpu.make_async_copy(src, dst, sem).start()

    def arrived(ref, sem):
        pltpu.make_async_copy(ref, ref, sem).wait()

    for p in range(NP):
        src, q = (panel_hbm, p) if p < PA else (channels_hbm, p - PA)
        bring(src.at[:, :, pl.ds(q * L, L)], own.at[p], local_sem.at[p])
    bring(inverses_hbm, inverses, local_sem.at[6])
    bring(coupling_hbm, coupling, local_sem.at[7])
    bring(front_hbm, front, local_sem.at[8])

    barrier = pltpu.get_barrier_semaphore()

    def greet(dev):
        pl.semaphore_signal(barrier, inc=1, device_id=dev, device_id_type=MESH)

    greet(sibling)
    for zz in range(NZ):

        @pl.when(jnp.logical_not(jnp.logical_and(on_diagonal, zz == z)))
        def _():
            greet(at(z, x, zz, k))

    near = 2 * k + 1 - odd
    for kk in range(2):
        greet(at(y, near, z, kk))

    def plane_peer(axis, d, e):
        xx = up(x, e, NX)
        if axis == "y":
            return at(up(y, d, NY), xx, z, k)
        return at(y, xx, up(z, d, NZ), k)

    def for_plane(one):
        for e in range(1, NX):
            one(e, 0, e)

        def step(d, carry):
            for e in range(NX):
                one(d * NX + e, d, e)
            return carry

        lax.fori_loop(1, NY, step, 0)

    def greet_plane(axis):
        for_plane(lambda n, d, e: greet(plane_peer(axis, d, e)))

    greet_plane("y")
    greet_plane("z")
    n_yz = jnp.where(on_diagonal, NY - 1, NY)
    pl.semaphore_wait(barrier, 1 + n_yz + 2 + 2 * (MEMBERS - 1))

    for p in range(NP):
        arrived(own.at[p], local_sem.at[p])

    near_first = (0, 1, 7, 2, 6, 3, 5, 4)

    def g_send(p):
        dst = mine.at[p, :, z]
        for d in near_first[1:]:
            send(own.at[p], dst, g_s.at[p], g_r.at[p], at(up(y, d, NY), x, y, k))

        @pl.when(on_diagonal)
        def _():
            bring(own.at[p], dst, g_r.at[p])

        @pl.when(jnp.logical_not(on_diagonal))
        def _():
            send(own.at[p], dst, g_s.at[p], g_r.at[p], at(y, x, y, k))

    def g_drain(p):
        arrived(mine.at[p, :, pl.ds(0, NY - 1)], g_s.at[p])

        @pl.when(jnp.logical_not(on_diagonal))
        def _():
            arrived(own.at[p], g_s.at[p])

    def x_step(p):
        arrived(mine.at[p], g_r.at[p])
        dst, sem = col.at[p, odd, :, :, k], x_r.at[p, odd, k]
        send(mine.at[p], dst, x_s.at[p], sem, at(y, up(x, 1, NX), z, user))
        send(mine.at[p], dst, x_s.at[p], sem, at(y, up(x, -1, NX), z, user))

        @pl.when(user == k)
        def _():
            bring(mine.at[p], dst, sem)

        @pl.when(user != k)
        def _():
            send(mine.at[p], dst, x_s.at[p], sem, sibling)

    def x_drain(p):
        arrived(mine.at[p], x_s.at[p])
        arrived(mine.at[p], x_s.at[p])

        @pl.when(user != k)
        def _():
            arrived(mine.at[p], x_s.at[p])

    from_left = near == up(x, -1, NX)
    h = jnp.where(from_left, 0, 1)
    beyond = at(y, jnp.where(from_left, up(x, 1, NX), up(x, -1, NX)), z, k)

    def x_forward(p):
        for kk in range(2):
            arrived(mine.at[p], x_r.at[p, 1 - odd, kk])
        part_ = col.at[p, 1 - odd, :, pl.ds(h * (NZ // 2), NZ // 2)]
        send(part_, part_, f_s.at[p], x_r.at[p, 1 - odd, h], beyond)

    def x_wait(p):
        for kk in range(2):
            arrived(mine.at[p], x_r.at[p, odd, kk])

    def f_drain(p):
        arrived(mine.at[p], f_s.at[p])

    spans = (pl.ds(0, PA), pl.ds(PA, PC))

    def along_z(d):
        return at(y, x, up(z, d, NZ), k)

    def row_part(g, zz, comp=None):
        if comp is None:
            return row.at[spans[g], :, zz, k]
        return row.at[spans[g], comp, zz, k]

    def row_own(g):
        bring(own.at[spans[g]], row_part(g, z), local_sem.at[9 + g])
        send(own.at[spans[g]], row_part(g, z), w_s.at[g, 0, 0], w_r.at[g, 0, 0], along_z(1))
        send(own.at[spans[g]], row_part(g, z), w_s.at[g, 0, 1], w_r.at[g, 0, 1], along_z(-1))

    def row_ring(g, step):
        for way, sign in ((0, 1), (1, -1)):
            zz = up(z, -sign * step, NZ)
            arrived(row_part(g, zz), w_r.at[g, step - 1, way])
            part_ = row_part(g, zz, way if step == 3 else None)
            send(part_, part_, w_s.at[g, step, way], w_r.at[g, step, way], along_z(sign))

    def row_sib(g):
        for way in (0, 1):
            arrived(row_part(g, up(z, 4, NZ), way), w_r.at[g, 3, way])
        arrived(own.at[spans[g]], local_sem.at[9 + g])
        both = row.at[spans[g], :, :, k]
        send(both, both, wc_s.at[g], wc_r.at[g], sibling)

    def row_wait(g):
        arrived(row.at[spans[g], :, :, other], wc_r.at[g])

    def row_drain(g):
        for step in range(4):
            for way in (0, 1):
                comp = way if step == 3 else None
                arrived(row_part(g, z, comp), w_s.at[g, step, way])
        arrived(row.at[spans[g], :, :, k], wc_s.at[g])

    def make_g():
        arrived(inverses, local_sem.at[6])
        arrived(coupling, local_sem.at[7])
        inv0 = (inverses[0, 0], inverses[0, 1])
        inv1 = (inverses[1, 0], inverses[1, 1])
        m = chdot(inv0, (coupling[0], coupling[1]), nt=True)
        n = chdot(m, inv1)
        nm = chdot(n, m, nt=True)
        im = chdot(inv1, m, nt=True)

        def block(i):
            top = jnp.concatenate([inv0[i] + nm[i], -n[i]], axis=1)
            return jnp.concatenate([top, jnp.concatenate([-im[i], inv1[i]], axis=1)], axis=0)

        gr, gi = block(0), block(1)
        return jnp.concatenate(
            [jnp.concatenate([gr, gi], axis=1), jnp.concatenate([-gi, gr], axis=1)], axis=0
        )

    def row_cat():
        parts = [row[p, i].reshape(NZ * 2 * 16, L) for i in range(2) for p in range(PA)]
        return jnp.concatenate(parts, axis=1)

    def make_scaled(g):
        scaled = hdot(row_cat(), g)
        xr, xi = scaled[:, : PA * L], scaled[:, PA * L :]
        both = jnp.concatenate(
            [jnp.concatenate([xr, -xi], axis=1), jnp.concatenate([xi, xr], axis=1)], axis=0
        )
        x_hi[...], x_lo[...] = split(both)

    def make_schur():
        for l in range(2):
            parts = [col[p, l, i].reshape(256, L) for i in range(2) for p in range(PA)]
            a = split(jnp.concatenate(parts, axis=1))
            update = dot3((x_hi[...], x_lo[...]), a, nt=True)
            for i in range(2):
                s = front[i, :, l * 256 : (l + 1) * 256] - update[i * 256 : (i + 1) * 256]
                schur[i, :, l * 256 : (l + 1) * 256] = s
                hi, lo = split(s)
                s_hi[i * 256 : (i + 1) * 256, l * 256 : (l + 1) * 256] = hi
                s_lo[i * 256 : (i + 1) * 256, l * 256 : (l + 1) * 256] = lo

    def make_ct():
        for i in range(2):
            for j in range(PC):
                t = row[PA + j, i].reshape(256, L).T
                hi, lo = split(t)
                ct_hi[i * 512 + j * L : i * 512 + (j + 1) * L] = hi
                ct_lo[i * 512 + j * L : i * 512 + (j + 1) * L] = lo

    def make_part(j):
        p = PA + j
        lines = []
        for l in range(2):
            lines.append(jnp.concatenate([col[p, l, i].reshape(256, L) for i in range(2)], axis=1))
        b = split(jnp.concatenate(lines, axis=0))
        t = dot3((s_hi[...], s_lo[...]), b)
        ar = t[:256, :L] - t[256:, L:]
        ai = t[:256, L:] + t[256:, :L]
        q = dot3((ct_hi[...], ct_lo[...]), split(jnp.concatenate([ar, ai], axis=1)))
        part[j, 0] = q[:512, :L] - q[512:, L:]
        part[j, 1] = q[:512, L:] + q[512:, :L]

    position = {"y": y * NX + x, "z": z * NX + x}
    along = {"y": y, "z": z}

    def rows(h, i):
        return pl.ds(pl.multiple_of(h * 256 + i * SLICE, SLICE), SLICE)

    def p_sib(j):
        send(part.at[j, other], sib_in.at[j], ps_s.at[j], ps_r.at[j], sibling)

    def rs(j):
        arrived(sib_in.at[j], ps_r.at[j])
        acc[j] = part[j, k] + sib_in[j]

        def one(n, d, e):
            for h, axis in enumerate(PLANES):
                to = up(along[axis], d, NY) * NX + up(x, e, NX)
                send(
                    acc.at[j, rows(h, to)], scat.at[j, h, n], rs_s.at[j], rs_r.at[j, h],
                    plane_peer(axis, d, e),
                )

        for_plane(one)

    def exchange(j):
        for h, axis in enumerate(PLANES):
            arrived(scat.at[j, h, pl.ds(1, MEMBERS - 1)], rs_r.at[j, h])
            total = acc[j, rows(h, position[axis])]
            for n in range(1, MEMBERS):
                total = total + scat[j, h, n]
            i = z if axis == "y" else y
            exch[j, h, i] = total
            mine_ = exch.at[j, h, i]
            for d in (1, 7, 2, 6, 3, 5, 4):
                dev = at(y, x, up(z, d, NZ), k) if axis == "y" else at(up(y, d, NY), x, z, k)
                send(mine_, mine_, e_s.at[j], e_r.at[j, h], dev)

    def ag(j):
        for h, axis in enumerate(PLANES):
            arrived(exch.at[j, h, pl.ds(0, NZ - 1)], e_r.at[j, h])
            total = exch[j, h, 0]
            for i in range(1, NZ):
                total = total + exch[j, h, i]
            whole[j, k, rows(h, position[axis])] = total

        def one(n, d, e):
            for h, axis in enumerate(PLANES):
                mine_ = whole.at[j, k, rows(h, position[axis])]
                send(mine_, mine_, ag_s.at[j], ag_r.at[j], plane_peer(axis, d, e))

        for_plane(one)

    def out(j, kk):
        return pltpu.make_async_copy(
            whole.at[j, kk], proj_hbm.at[kk, :, pl.ds(j * L, L)], out_sem.at[j, kk]
        )

    def fin(j):
        arrived(scat.at[j, :, pl.ds(1, MEMBERS - 1)], ag_r.at[j])
        send(whole.at[j, k], whole.at[j, k], fin_s.at[j], fin_r.at[j], sibling)
        out(j, k).start()

    def fin_wait(j):
        arrived(whole.at[j, other], fin_r.at[j])
        out(j, other).start()

    def sum_drain(j):
        arrived(sib_in.at[j], ps_s.at[j])
        arrived(sib_in.at[j], fin_s.at[j])
        arrived(scat.at[j, :, pl.ds(1, MEMBERS - 1)], rs_s.at[j])
        arrived(scat.at[j, :, pl.ds(1, MEMBERS - 1)], ag_s.at[j])
        arrived(exch.at[j, :, pl.ds(0, NZ - 1)], e_s.at[j])

    g_send(0)
    g_send(1)
    row_own(0)
    g = make_g()
    x_step(0)
    g_send(2)
    row_ring(0, 1)
    x_step(1)
    g_send(3)
    row_ring(0, 2)
    row_own(1)
    x_step(2)
    x_forward(0)
    g_send(4)
    row_ring(0, 3)
    x_step(3)
    x_forward(1)
    g_send(5)
    row_ring(1, 1)
    row_sib(0)
    x_step(4)
    x_forward(2)
    row_ring(1, 2)
    row_wait(0)
    make_scaled(g)
    x_step(5)
    x_forward(3)
    row_ring(1, 3)
    x_wait(0)
    x_wait(1)
    arrived(front, local_sem.at[8])
    make_schur()
    bring(schur, schur_hbm, local_sem.at[11])
    row_sib(1)
    x_forward(4)
    x_wait(2)
    row_wait(1)
    make_ct()
    make_part(0)
    p_sib(0)
    x_wait(3)
    make_part(1)
    p_sib(1)
    rs(0)
    x_forward(5)
    x_wait(4)
    make_part(2)
    p_sib(2)
    rs(1)
    exchange(0)
    rs(2)
    x_wait(5)
    make_part(3)
    p_sib(3)
    exchange(1)
    ag(0)
    rs(3)
    exchange(2)
    ag(1)
    exchange(3)
    ag(2)
    fin(0)
    ag(3)
    fin(1)
    fin_wait(0)
    fin(2)
    fin_wait(1)
    fin(3)
    fin_wait(2)
    fin_wait(3)

    for p in range(NP):
        g_drain(p)
        x_drain(p)
        f_drain(p)
    for q in range(2):
        row_drain(q)
    for j in range(PC):
        sum_drain(j)
    arrived(schur, local_sem.at[11])
    for j in range(PC):
        for kk in range(2):
            out(j, kk).wait()


def local(front, panel, inverses, coupling, channels):
    hbm = pl.BlockSpec(memory_space=pltpu.HBM)
    dma = pltpu.SemaphoreType.DMA
    v = pltpu.VMEM
    scratch = [
        v((2, 256, 512), F32),
        v((2, 256, 512), F32),
        v((2, 2, 128, 128), F32),
        v((2, 128, 128), F32),
        v((NP, 2, 16, L), F32),
        v((NP, 2, NZ, 16, L), F32),
        v((NP, 2, 2, NZ, 2, 16, L), F32),
        v((NP, 2, NZ, 2, 16, L), F32),
        v((512, 512), BF16), v((512, 512), BF16),
        v((1024, 256), BF16), v((1024, 256), BF16),
        v((512, 512), BF16), v((512, 512), BF16),
        v((PC, 2, 512, L), F32),
        v((PC, 512, L), F32), v((PC, 512, L), F32),
        v((PC, 2, MEMBERS, SLICE, L), F32),
        v((PC, 2, NZ, SLICE, L), F32),
        v((PC, 2, 512, L), F32),
        dma((NP,)), dma((NP,)),
        dma((NP,)), dma((NP, 2, 2)), dma((NP,)),
        dma((2, 4, 2)), dma((2, 4, 2)), dma((2,)), dma((2,)),
        dma((PC,)), dma((PC,)), dma((PC,)), dma((PC, 2)), dma((PC,)), dma((PC, 2)),
        dma((PC,)), dma((PC,)), dma((PC,)), dma((PC,)),
        dma((12,)), dma((PC, 2)),
    ]
    return pl.pallas_call(
        kernel,
        out_shape=(
            jax.ShapeDtypeStruct((2, 256, 512), F32),
            jax.ShapeDtypeStruct((2, 512, 512), F32),
        ),
        in_specs=[hbm] * 5,
        out_specs=(hbm, hbm),
        scratch_shapes=scratch,
        compiler_params=pltpu.CompilerParams(
            collective_id=0, has_side_effects=True, vmem_limit_bytes=56 * 2**20
        ),
        cost_estimate=pl.CostEstimate(flops=4 * 10**9, bytes_accessed=8 * 2**20, transcendentals=0),
    )(front, panel, inverses, coupling, channels)


def solution(mesh):
    in_specs = (P(None, "row", "col"), P(None, ("row", "col"), None), P(), P(), P(None, ("row", "col"), None))
    out_specs = (P(None, "row", "col"), P())
    return jax.shard_map(local, mesh=mesh, in_specs=in_specs, out_specs=out_specs, check_vma=False)
```

```python
import functools

import jax
import jax.numpy as jnp
from jax import lax
from jax.experimental import pallas as pl
from jax.experimental.pallas import tpu as pltpu
from jax.sharding import PartitionSpec as P

MESH = pl.DeviceIdType.MESH
HIGH = lax.Precision.HIGHEST
F32 = jnp.float32
BF16 = jnp.bfloat16
NY, NX, NZ = 8, 4, 8
PA, PC = 2, 4
NP = PA + PC
L = 128
PLANES = ("y", "z")
MEMBERS = 32
SLICE = 256 // MEMBERS


def split(v):
    hi = v.astype(BF16)
    return hi, (v - hi.astype(F32)).astype(BF16)


def bdot(a, b, nt=False):
    dims = (((1,), (1 if nt else 0,)), ((), ()))
    return lax.dot_general(a, b, dims, preferred_element_type=F32)


def dot3(a, b, nt=False):
    (ah, al), (bh, bl) = a, b
    return bdot(ah, bh, nt) + (bdot(ah, bl, nt) + bdot(al, bh, nt))


def hdot(a, b, nt=False):
    dims = (((1,), (1 if nt else 0,)), ((), ()))
    return lax.dot_general(a, b, dims, precision=HIGH, preferred_element_type=F32)


def chdot(a, b, nt=False):
    (ar, ai), (br, bi) = a, b
    return (
        hdot(ar, br, nt) - hdot(ai, bi, nt),
        hdot(ar, bi, nt) + hdot(ai, br, nt),
    )


def kernel(
    front_hbm, panel_hbm, inverses_hbm, coupling_hbm, channels_hbm, schur_hbm, proj_hbm,
    front, schur, inverses, coupling, own, mine, col, row, s_hi, s_lo, ct_hi, ct_lo, x_hi, x_lo,
    part, sib_in, acc, scat, exch, whole,
    g_s, g_r, x_s, x_r, f_s, w_s, w_r, wc_s, wc_r,
    ps_s, ps_r, rs_s, rs_r, e_s, e_r, ag_s, ag_r, fin_s, fin_r, local_sem, out_sem,
):
    r = lax.axis_index("row")
    c = lax.axis_index("col")
    y, x, z, k = r // NX, lax.rem(r, NX), c // 2, lax.rem(c, 2)
    other = 1 - k

    def at(yy, xx, zz, kk):
        return (yy * NX + xx, zz * 2 + kk)

    def up(v, d, n):
        return lax.rem(v + (d + n), n)

    sibling = at(y, x, z, other)
    user = x // 2
    odd = lax.rem(x, 2)
    on_diagonal = y == z

    def send(src, dst, s, r_, dev):
        copy = pltpu.make_async_remote_copy(
            src_ref=src, dst_ref=dst, send_sem=s, recv_sem=r_, device_id=dev, device_id_type=MESH
        )
        copy.start()

    def bring(src, dst, sem):
        pltpu.make_async_copy(src, dst, sem).start()

    def arrived(ref, sem):
        pltpu.make_async_copy(ref, ref, sem).wait()

    for p in range(NP):
        src, q = (panel_hbm, p) if p < PA else (channels_hbm, p - PA)
        bring(src.at[:, :, pl.ds(q * L, L)], own.at[p], local_sem.at[p])
    bring(inverses_hbm, inverses, local_sem.at[6])
    bring(coupling_hbm, coupling, local_sem.at[7])
    bring(front_hbm, front, local_sem.at[8])

    barrier = pltpu.get_barrier_semaphore()

    def greet(dev):
        pl.semaphore_signal(barrier, inc=1, device_id=dev, device_id_type=MESH)

    greet(sibling)
    for zz in range(NZ):

        @pl.when(jnp.logical_not(jnp.logical_and(on_diagonal, zz == z)))
        def _():
            greet(at(z, x, zz, k))

    near = 2 * k + 1 - odd
    for kk in range(2):
        greet(at(y, near, z, kk))

    def plane_peer(axis, d, e):
        xx = up(x, e, NX)
        if axis == "y":
            return at(up(y, d, NY), xx, z, k)
        return at(y, xx, up(z, d, NZ), k)

    def for_plane(one):
        for e in range(1, NX):
            one(e, 0, e)

        def step(d, carry):
            for e in range(NX):
                one(d * NX + e, d, e)
            return carry

        lax.fori_loop(1, NY, step, 0)

    def greet_plane(axis):
        for_plane(lambda n, d, e: greet(plane_peer(axis, d, e)))

    greet_plane("y")
    greet_plane("z")
    n_yz = jnp.where(on_diagonal, NY - 1, NY)
    pl.semaphore_wait(barrier, 1 + n_yz + 2 + 2 * (MEMBERS - 1))

    for p in range(NP):
        arrived(own.at[p], local_sem.at[p])

    near_first = (0, 1, 7, 2, 6, 3, 5, 4)

    def g_send(p):
        dst = mine.at[p, :, z]
        for d in near_first[1:]:
            send(own.at[p], dst, g_s.at[p], g_r.at[p], at(up(y, d, NY), x, y, k))

        @pl.when(on_diagonal)
        def _():
            bring(own.at[p], dst, g_r.at[p])

        @pl.when(jnp.logical_not(on_diagonal))
        def _():
            send(own.at[p], dst, g_s.at[p], g_r.at[p], at(y, x, y, k))

    def g_drain(p):
        arrived(mine.at[p, :, pl.ds(0, NY - 1)], g_s.at[p])

        @pl.when(jnp.logical_not(on_diagonal))
        def _():
            arrived(own.at[p], g_s.at[p])

    def x_step(p):
        arrived(mine.at[p], g_r.at[p])
        dst, sem = col.at[p, odd, :, :, k], x_r.at[p, odd, k]
        send(mine.at[p], dst, x_s.at[p], sem, at(y, up(x, 1, NX), z, user))
        send(mine.at[p], dst, x_s.at[p], sem, at(y, up(x, -1, NX), z, user))

        @pl.when(user == k)
        def _():
            bring(mine.at[p], dst, sem)

        @pl.when(user != k)
        def _():
            send(mine.at[p], dst, x_s.at[p], sem, sibling)

    def x_drain(p):
        arrived(mine.at[p], x_s.at[p])
        arrived(mine.at[p], x_s.at[p])

        @pl.when(user != k)
        def _():
            arrived(mine.at[p], x_s.at[p])

    from_left = near == up(x, -1, NX)
    h = jnp.where(from_left, 0, 1)
    beyond = at(y, jnp.where(from_left, up(x, 1, NX), up(x, -1, NX)), z, k)

    def x_forward(p):
        for kk in range(2):
            arrived(mine.at[p], x_r.at[p, 1 - odd, kk])
        part_ = col.at[p, 1 - odd, :, pl.ds(h * (NZ // 2), NZ // 2)]
        send(part_, part_, f_s.at[p], x_r.at[p, 1 - odd, h], beyond)

    def x_wait(p):
        for kk in range(2):
            arrived(mine.at[p], x_r.at[p, odd, kk])

    def f_drain(p):
        arrived(mine.at[p], f_s.at[p])

    spans = (pl.ds(0, PA), pl.ds(PA, PC))

    def along_z(d):
        return at(y, x, up(z, d, NZ), k)

    def row_part(g, zz, comp=None):
        if comp is None:
            return row.at[spans[g], :, zz, k]
        return row.at[spans[g], comp, zz, k]

    def row_own(g):
        bring(own.at[spans[g]], row_part(g, z), local_sem.at[9 + g])
        send(own.at[spans[g]], row_part(g, z), w_s.at[g, 0, 0], w_r.at[g, 0, 0], along_z(1))
        send(own.at[spans[g]], row_part(g, z), w_s.at[g, 0, 1], w_r.at[g, 0, 1], along_z(-1))

    def row_ring(g, step):
        for way, sign in ((0, 1), (1, -1)):
            zz = up(z, -sign * step, NZ)
            arrived(row_part(g, zz), w_r.at[g, step - 1, way])
            part_ = row_part(g, zz, way if step == 3 else None)
            send(part_, part_, w_s.at[g, step, way], w_r.at[g, step, way], along_z(sign))

    def row_sib(g):
        for way in (0, 1):
            arrived(row_part(g, up(z, 4, NZ), way), w_r.at[g, 3, way])
        arrived(own.at[spans[g]], local_sem.at[9 + g])
        both = row.at[spans[g], :, :, k]
        send(both, both, wc_s.at[g], wc_r.at[g], sibling)

    def row_wait(g):
        arrived(row.at[spans[g], :, :, other], wc_r.at[g])

    def row_drain(g):
        for step in range(4):
            for way in (0, 1):
                comp = way if step == 3 else None
                arrived(row_part(g, z, comp), w_s.at[g, step, way])
        arrived(row.at[spans[g], :, :, k], wc_s.at[g])

    def make_g():
        arrived(inverses, local_sem.at[6])
        arrived(coupling, local_sem.at[7])
        inv0 = (inverses[0, 0], inverses[0, 1])
        inv1 = (inverses[1, 0], inverses[1, 1])
        m = chdot(inv0, (coupling[0], coupling[1]), nt=True)
        n = chdot(m, inv1)
        nm = chdot(n, m, nt=True)
        im = chdot(inv1, m, nt=True)

        def block(i):
            top = jnp.concatenate([inv0[i] + nm[i], -n[i]], axis=1)
            return jnp.concatenate([top, jnp.concatenate([-im[i], inv1[i]], axis=1)], axis=0)

        gr, gi = block(0), block(1)
        return jnp.concatenate(
            [jnp.concatenate([gr, gi], axis=1), jnp.concatenate([-gi, gr], axis=1)], axis=0
        )

    def row_cat():
        parts = [row[p, i].reshape(NZ * 2 * 16, L) for i in range(2) for p in range(PA)]
        return jnp.concatenate(parts, axis=1)

    def make_scaled(g):
        scaled = hdot(row_cat(), g)
        xr, xi = scaled[:, : PA * L], scaled[:, PA * L :]
        both = jnp.concatenate(
            [jnp.concatenate([xr, -xi], axis=1), jnp.concatenate([xi, xr], axis=1)], axis=0
        )
        x_hi[...], x_lo[...] = split(both)

    def make_schur():
        for l in range(2):
            parts = [col[p, l, i].reshape(256, L) for i in range(2) for p in range(PA)]
            a = split(jnp.concatenate(parts, axis=1))
            update = dot3((x_hi[...], x_lo[...]), a, nt=True)
            for i in range(2):
                s = front[i, :, l * 256 : (l + 1) * 256] - update[i * 256 : (i + 1) * 256]
                schur[i, :, l * 256 : (l + 1) * 256] = s
                hi, lo = split(s)
                s_hi[i * 256 : (i + 1) * 256, l * 256 : (l + 1) * 256] = hi
                s_lo[i * 256 : (i + 1) * 256, l * 256 : (l + 1) * 256] = lo

    def make_ct():
        for i in range(2):
            for j in range(PC):
                t = row[PA + j, i].reshape(256, L).T
                hi, lo = split(t)
                ct_hi[i * 512 + j * L : i * 512 + (j + 1) * L] = hi
                ct_lo[i * 512 + j * L : i * 512 + (j + 1) * L] = lo

    def make_part(j):
        p = PA + j
        lines = []
        for l in range(2):
            lines.append(jnp.concatenate([col[p, l, i].reshape(256, L) for i in range(2)], axis=1))
        b = split(jnp.concatenate(lines, axis=0))
        t = dot3((s_hi[...], s_lo[...]), b)
        ar = t[:256, :L] - t[256:, L:]
        ai = t[:256, L:] + t[256:, :L]
        q = dot3((ct_hi[...], ct_lo[...]), split(jnp.concatenate([ar, ai], axis=1)))
        part[j, 0] = q[:512, :L] - q[512:, L:]
        part[j, 1] = q[:512, L:] + q[512:, :L]

    position = {"y": y * NX + x, "z": z * NX + x}
    along = {"y": y, "z": z}

    def rows(h, i):
        return pl.ds(pl.multiple_of(h * 256 + i * SLICE, SLICE), SLICE)

    def p_sib(j):
        send(part.at[j, other], sib_in.at[j], ps_s.at[j], ps_r.at[j], sibling)

    def rs(j):
        arrived(sib_in.at[j], ps_r.at[j])
        acc[j] = part[j, k] + sib_in[j]

        def one(n, d, e):
            for h, axis in enumerate(PLANES):
                to = up(along[axis], d, NY) * NX + up(x, e, NX)
                send(
                    acc.at[j, rows(h, to)], scat.at[j, h, n], rs_s.at[j], rs_r.at[j, h],
                    plane_peer(axis, d, e),
                )

        for_plane(one)

    def exchange(j):
        for h, axis in enumerate(PLANES):
            arrived(scat.at[j, h, pl.ds(1, MEMBERS - 1)], rs_r.at[j, h])
            total = acc[j, rows(h, position[axis])]
            for n in range(1, MEMBERS):
                total = total + scat[j, h, n]
            i = z if axis == "y" else y
            exch[j, h, i] = total
            mine_ = exch.at[j, h, i]
            for d in (1, 7, 2, 6, 3, 5, 4):
                dev = at(y, x, up(z, d, NZ), k) if axis == "y" else at(up(y, d, NY), x, z, k)
                send(mine_, mine_, e_s.at[j], e_r.at[j, h], dev)

    def ag(j):
        for h, axis in enumerate(PLANES):
            arrived(exch.at[j, h, pl.ds(0, NZ - 1)], e_r.at[j, h])
            total = exch[j, h, 0]
            for i in range(1, NZ):
                total = total + exch[j, h, i]
            whole[j, k, rows(h, position[axis])] = total

        def one(n, d, e):
            for h, axis in enumerate(PLANES):
                mine_ = whole.at[j, k, rows(h, position[axis])]
                send(mine_, mine_, ag_s.at[j], ag_r.at[j], plane_peer(axis, d, e))

        for_plane(one)

    def out_place(j):
        return proj_hbm.at[k, :, pl.ds(j * L, L)]

    def out(j):
        return pltpu.make_async_copy(whole.at[j, k], out_place(j), out_sem.at[j])

    def fin(j):
        arrived(scat.at[j, :, pl.ds(1, MEMBERS - 1)], ag_r.at[j])
        send(whole.at[j, k], out_place(j), fin_s.at[j], fin_r.at[j], sibling)
        out(j).start()

    def fin_wait(j):
        arrived(sib_in.at[j], fin_r.at[j])

    def sum_drain(j):
        arrived(sib_in.at[j], ps_s.at[j])
        arrived(sib_in.at[j], fin_s.at[j])
        arrived(scat.at[j, :, pl.ds(1, MEMBERS - 1)], rs_s.at[j])
        arrived(scat.at[j, :, pl.ds(1, MEMBERS - 1)], ag_s.at[j])
        arrived(exch.at[j, :, pl.ds(0, NZ - 1)], e_s.at[j])

    g_send(0)
    g_send(1)
    row_own(0)
    g = make_g()
    x_step(0)
    g_send(2)
    row_ring(0, 1)
    x_step(1)
    g_send(3)
    row_ring(0, 2)
    row_own(1)
    x_step(2)
    x_forward(0)
    g_send(4)
    row_ring(0, 3)
    x_step(3)
    x_forward(1)
    g_send(5)
    row_ring(1, 1)
    row_sib(0)
    x_step(4)
    x_forward(2)
    row_ring(1, 2)
    row_wait(0)
    make_scaled(g)
    x_step(5)
    x_forward(3)
    row_ring(1, 3)
    x_wait(0)
    x_wait(1)
    arrived(front, local_sem.at[8])
    make_schur()
    bring(schur, schur_hbm, local_sem.at[11])
    row_sib(1)
    x_forward(4)
    x_wait(2)
    row_wait(1)
    make_ct()
    make_part(0)
    p_sib(0)
    x_wait(3)
    make_part(1)
    p_sib(1)
    rs(0)
    x_forward(5)
    x_wait(4)
    make_part(2)
    p_sib(2)
    rs(1)
    exchange(0)
    rs(2)
    x_wait(5)
    make_part(3)
    p_sib(3)
    exchange(1)
    rs(3)
    ag(0)
    exchange(2)
    ag(1)
    exchange(3)
    ag(2)
    ag(3)
    fin(0)
    fin(1)
    fin(2)
    fin(3)
    fin_wait(0)
    fin_wait(1)
    fin_wait(2)
    fin_wait(3)

    for p in range(NP):
        g_drain(p)
        x_drain(p)
        f_drain(p)
    for q in range(2):
        row_drain(q)
    for j in range(PC):
        sum_drain(j)
    arrived(schur, local_sem.at[11])
    for j in range(PC):
        out(j).wait()


def local(front, panel, inverses, coupling, channels):
    hbm = pl.BlockSpec(memory_space=pltpu.HBM)
    dma = pltpu.SemaphoreType.DMA
    v = pltpu.VMEM
    scratch = [
        v((2, 256, 512), F32),
        v((2, 256, 512), F32),
        v((2, 2, 128, 128), F32),
        v((2, 128, 128), F32),
        v((NP, 2, 16, L), F32),
        v((NP, 2, NZ, 16, L), F32),
        v((NP, 2, 2, NZ, 2, 16, L), F32),
        v((NP, 2, NZ, 2, 16, L), F32),
        v((512, 512), BF16), v((512, 512), BF16),
        v((1024, 256), BF16), v((1024, 256), BF16),
        v((512, 512), BF16), v((512, 512), BF16),
        v((PC, 2, 512, L), F32),
        v((PC, 512, L), F32), v((PC, 512, L), F32),
        v((PC, 2, MEMBERS, SLICE, L), F32),
        v((PC, 2, NZ, SLICE, L), F32),
        v((PC, 2, 512, L), F32),
        dma((NP,)), dma((NP,)),
        dma((NP,)), dma((NP, 2, 2)), dma((NP,)),
        dma((2, 4, 2)), dma((2, 4, 2)), dma((2,)), dma((2,)),
        dma((PC,)), dma((PC,)), dma((PC,)), dma((PC, 2)), dma((PC,)), dma((PC, 2)),
        dma((PC,)), dma((PC,)), dma((PC,)), dma((PC,)),
        dma((12,)), dma((PC,)),
    ]
    return pl.pallas_call(
        kernel,
        out_shape=(
            jax.ShapeDtypeStruct((2, 256, 512), F32),
            jax.ShapeDtypeStruct((2, 512, 512), F32),
        ),
        in_specs=[hbm] * 5,
        out_specs=(hbm, hbm),
        scratch_shapes=scratch,
        compiler_params=pltpu.CompilerParams(
            collective_id=0, has_side_effects=True, vmem_limit_bytes=56 * 2**20
        ),
        cost_estimate=pl.CostEstimate(flops=4 * 10**9, bytes_accessed=8 * 2**20, transcendentals=0),
    )(front, panel, inverses, coupling, channels)


def solution(mesh):
    in_specs = (P(None, "row", "col"), P(None, ("row", "col"), None), P(), P(), P(None, ("row", "col"), None))
    out_specs = (P(None, "row", "col"), P())
    return jax.shard_map(local, mesh=mesh, in_specs=in_specs, out_specs=out_specs, check_vma=False)
```
